512 devices in a mesh: tm: 16 (over x_lo, y), space: 32 (over x_hi, z, core).
Axes of the slice: x: 4 (x_hi: 2, x_lo: 2; x = x_hi * 2 + x_lo), y: 8, z: 8, core: 2. Of those that a mesh axis runs over, the one named last changes fastest.
Arguments:
- adjoint_start: float32 [32, 5, 192, 2048], P('tm', None, 'space'), may hold values from -6 to 6
- source: float32 [32, 5, 192, 2048], P('tm', None, 'space'), may hold values from -6 to 6
- inv_diagonal: bfloat16 [5, 5, 192, 2048], P(None, None, 'space'), may hold values from -0.081 to 0.35
- east_block: bfloat16 [5, 5, 192, 2048], P(None, None, 'space'), may hold values from -1.796875 to 1.796875
- west_block: bfloat16 [5, 5, 192, 2048], P(None, None, 'space'), may hold values from -1.796875 to 1.796875
- pair_block: bfloat16 [5, 5, 192, 2048], P(None, None, 'space'), may hold values from -1.796875 to 1.796875
- time_scale: float32 [192, 2048], P('space'), may hold values from 0.02 to 0.2
- partner: int32 [192, 2048], P('space'), may hold values from 0 to 5, as said below
Outputs:
- adjoint: float32 [32, 5, 192, 2048], P('tm', None, 'space')
The draws below stay inside these ranges and needn't reach their ends.
Inputs may be any that keep to these rules, and one draw needn't show every extreme that they name: In each column r and each block of 6 cells along the first dimension starting at a multiple of 6, partner pairs the block's cells: the partner of a cell's partner is the cell itself, and no cell is its own partner.
All inputs are finite; a program needn't handle non-finite values.
Results may differ from the reference program's by a relative error of at most 0.0003.
Values sent between devices are 32-bit elements; how exact they have to be, the bound alone decides.
A program may use at most 64 MiB of HBM per device.

```python
import math
import jax
import jax.numpy as jnp
from jax import lax

VARS = 5
ITERS = 2
CX = 6
NR = 2048
INST = 32
NX = 192


def draw_inv_diagonal(key, part):
    key = jax.random.fold_in(key, 3)
    first, second = jax.random.split(key)
    identity = jnp.eye(5, dtype=jnp.float32)[:, :, None, None]
    diagonal = jnp.exp(jax.random.uniform(first, (5, NX, NR), jnp.float32, jnp.log(0.15), jnp.log(0.35)))
    offdiag = jnp.clip(0.035 * jax.random.normal(second, (5, 5, NX, NR), jnp.float32), -0.08, 0.08)
    result = identity * diagonal[:, None] + (1.0 - identity) * offdiag
    return result.astype(jnp.bfloat16)


def draw_partner(key, part):
    key = jax.random.fold_in(key, 7)
    blocks = NX // CX
    raw_scores = jax.random.randint(key, (blocks, CX, NR), 0, 1 << 20, jnp.int32)
    scores = raw_scores * CX + jnp.arange(CX, dtype=jnp.int32)[None, :, None]
    order = jnp.argsort(scores, axis=1).astype(jnp.int32)
    swapped = order.reshape(blocks, CX // 2, 2, NR)[:, :, ::-1].reshape(blocks, CX, NR)
    inverse = jnp.argsort(order, axis=1).astype(jnp.int32)
    paired = jnp.take_along_axis(swapped, inverse, axis=1)
    return paired.reshape(NX, NR).astype(jnp.int32)


def block_scale(stream_key, dims, cuts, least, largest):
    gain, own = 1.0, jax.random.fold_in(stream_key, 6)
    for position, shards_of in cuts:
        draws = jnp.exp(jax.random.uniform(jax.random.fold_in(own, position), (shards_of,), jnp.float32, least / len(cuts), largest / len(cuts)))
        gain = gain * jnp.repeat(draws, dims[position] // shards_of).reshape([-1 if axis == position else 1 for axis in range(len(dims))])
    return gain


def scatter_about(key, extent, width, bound, cuts=(), held_as=jnp.bfloat16):
    factor_of = block_scale(key, extent, cuts, -0.22, 0.18) if cuts else 1.0
    drawn = jax.random.normal(key, extent, jnp.float32) * width * factor_of
    return jnp.minimum(jnp.maximum(drawn, -bound), bound).astype(held_as)


def setup_inputs(seed: int = 0) -> dict:
    splits = jax.random.split(jax.random.key(seed), 9)
    adjoint_start = scatter_about(splits[0], (INST, VARS, NX, NR), 1.0, 6.0, ((0, 16), (2, 32)), jnp.float32)
    source = scatter_about(splits[1], (INST, VARS, NX, NR), 1.0, 6.0, ((0, 16), (2, 32)), jnp.float32)
    inv_diagonal = draw_inv_diagonal(jax.random.fold_in(splits[8], 71), 0)
    east_block = scatter_about(splits[3], (VARS, VARS, NX, NR), 0.3, 1.796875, ((2, 32),))
    west_block = scatter_about(splits[4], (VARS, VARS, NX, NR), 0.3, 1.796875, ((2, 32),))
    pair_block = scatter_about(splits[5], (VARS, VARS, NX, NR), 0.3, 1.796875, ((2, 32),))
    time_scale = jnp.clip(jnp.exp(math.log(0.2) - 2.3025851 * jax.random.uniform(splits[6], (NX, NR), jnp.float32) ** block_scale(splits[6], (NX, NR), ((0, 32),), -0.2, 0.2)), 0.02, 0.2)
    partner = draw_partner(jax.random.fold_in(splits[8], 71), 0)
    return dict(adjoint_start=adjoint_start, source=source, inv_diagonal=inv_diagonal, east_block=east_block, west_block=west_block, pair_block=pair_block, time_scale=time_scale, partner=partner)


def apply_transposed(matrix, vector):
    total = matrix[0][None].astype(jnp.float32) * vector[:, 0:1]
    for column in range(1, 5):
        total = total + matrix[column][None].astype(jnp.float32) * vector[:, column:column + 1]
    return total


def spectral_matrix(rows_global, cols_global, count):
    gap = jnp.mod(rows_global[:, None] - cols_global[None, :], count).astype(jnp.int32)
    angle = math.pi * gap.astype(jnp.float32) / count
    parity = (2 * jnp.mod(gap, 2) - 1).astype(jnp.float32)
    safe = jnp.where(gap == 0, 1.0, jnp.sin(angle))
    value = 0.5 * parity * jnp.cos(angle) / safe
    dead = jnp.logical_or(gap == 0, 2 * gap == count)
    return jnp.where(dead, 0.0, value).astype(jnp.float32)


def reference(adjoint_start, source, inv_diagonal, east_block, west_block, pair_block, time_scale, partner):
    offset = (jnp.arange(NX, dtype=jnp.int32) // CX * CX).astype(jnp.int32)[:, None]
    pcell = (partner + offset).astype(jnp.int32)
    every = jnp.arange(INST, dtype=jnp.int32)
    coupling = spectral_matrix(every, every, INST)
    adjoint = adjoint_start
    for iteration in range(ITERS):
        east_term = apply_transposed(east_block, adjoint)
        west_term = apply_transposed(west_block, adjoint)
        pair_term = apply_transposed(pair_block, adjoint)
        zero_row = jnp.zeros_like(east_term[:, :, :1])
        east_in = jnp.concatenate([zero_row, east_term[:, :, :-1]], axis=2)
        west_in = jnp.concatenate([west_term[:, :, 1:], zero_row], axis=2)
        pair_in = jnp.take_along_axis(pair_term, pcell[None, None], axis=2)
        offdiag = east_in + west_in + pair_in
        band_sum = jnp.einsum("nm,mvxr->nvxr", coupling, adjoint, precision=lax.Precision.HIGHEST)
        time_term = time_scale[None, None] * band_sum
        adjoint = apply_transposed(inv_diagonal, source - offdiag - time_term)
    return adjoint
```

```python
import math

import jax
import jax.numpy as jnp
from jax import lax
from jax.experimental import pallas as pl
from jax.experimental.pallas import tpu as pltpu
from jax.sharding import PartitionSpec as P

MESH = pl.DeviceIdType.MESH
TM = 16
RING = 8
SPACE = 32
INST = 32
OWN = INST // TM
VARS = 5
CX = 6
LANES = 128
ROWS = 8
BLOCK = 4

PEERS = [
    (across, along)
    for along in (4, 3, 5, 2, 6, 1, 7, 0)
    for across in (1, 0)
    if (across, along) != (0, 0)
]


def time_weights():
    return [
        0.0 if d in (0, INST // 2) else 0.5 * (-1) ** (d + 1) / math.tan(math.pi * d / INST)
        for d in range(INST)
    ]


def negacyclic(weights, value):
    count = len(weights)
    back = -value
    wide = jnp.concatenate([back, value, back], axis=0)
    half = count // 2
    total = weights[half] * wide[count - half : 2 * count - half]
    for d in range(1, half):
        total = total + weights[d] * (wide[count - d : 2 * count - d] - wide[count + d : 2 * count + d])
    return total


def cyclic(weights, value):
    count = len(weights)
    if count == 8:
        wide = jnp.concatenate([value, value, value], axis=0)
        total = None
        for d in range(1, count // 2):
            term = weights[d] * (wide[count - d : 2 * count - d] - wide[count + d : 2 * count + d])
            total = term if total is None else total + term
        return total
    half = count // 2
    low, high = value[:half], value[half:]
    plus = cyclic([0.5 * (weights[d] + weights[d + half]) for d in range(half)], low + high)
    minus = negacyclic([0.5 * (weights[d] - weights[d + half]) for d in range(half)], low - high)
    return jnp.concatenate([plus + minus, plus - minus], axis=0)


def kernel(
    start_hbm,
    source_hbm,
    inv_hbm,
    east_hbm,
    west_hbm,
    pair_hbm,
    scale_hbm,
    partner_hbm,
    out_hbm,
    first,
    source,
    second,
    offdiag,
    result,
    packed,
    blocks,
    scale,
    partner,
    east_out,
    west_out,
    east_in,
    west_in,
    local_sem,
    send_sem,
    recv_sem,
    halo_send,
    halo_recv,
    back_send,
    back_recv,
):
    tm, space = lax.axis_index("tm"), lax.axis_index("space")
    across, along = tm // RING, lax.rem(tm, RING)
    INV, EAST, WEST, PAIR = range(4)
    flat = lambda ref: ref.reshape(INST * VARS * ROWS, LANES)
    columns = lambda who: pl.ds(pl.multiple_of(who * LANES, LANES), LANES)
    cells = pl.ds(0, CX)

    own = []
    for slot, block_hbm in enumerate((inv_hbm, east_hbm, west_hbm, pair_hbm)):
        own.append(
            pltpu.make_async_copy(block_hbm.at[:, :, :, columns(tm)], packed.at[slot], local_sem.at[slot])
        )
    own.append(pltpu.make_async_copy(scale_hbm.at[:, columns(tm)], scale.at[cells], local_sem.at[4]))
    own.append(pltpu.make_async_copy(partner_hbm.at[:, columns(tm)], partner.at[cells], local_sem.at[5]))
    for slot, (field_hbm, field) in enumerate(((start_hbm, first), (source_hbm, source))):
        own.append(
            pltpu.make_async_copy(
                field_hbm.at[:, :, :, columns(tm)],
                field.at[pl.ds(tm * OWN, OWN), :, cells, :],
                local_sem.at[6 + slot],
            )
        )
    for copy in own:
        copy.start()

    barrier = pltpu.get_barrier_semaphore()
    peers = [
        lax.rem(across + da, 2) * RING + lax.rem(along + dy, RING) for da, dy in PEERS
    ]
    for peer in peers:
        pl.semaphore_signal(barrier, inc=1, device_id=(peer, space), device_id_type=MESH)
    has_next, has_previous = space < SPACE - 1, space > 0

    @pl.when(has_next)
    def _():
        pl.semaphore_signal(barrier, inc=1, device_id=(tm, space + 1), device_id_type=MESH)

    @pl.when(has_previous)
    def _():
        pl.semaphore_signal(barrier, inc=1, device_id=(tm, space - 1), device_id_type=MESH)

    pl.semaphore_wait(barrier, len(peers) + has_next.astype(jnp.int32) + has_previous.astype(jnp.int32))

    gathers = []
    for slot, (field_hbm, field) in enumerate(((start_hbm, first), (source_hbm, source))):
        copies = []
        for step, peer in enumerate(peers):
            copy = pltpu.make_async_remote_copy(
                src_ref=field_hbm.at[:, :, :, columns(peer)],
                dst_ref=field.at[pl.ds(tm * OWN, OWN), :, cells, :],
                send_sem=send_sem.at[slot, step],
                recv_sem=recv_sem.at[slot, step],
                device_id=(peer, space),
                device_id_type=MESH,
            )
            copy.start()
            copies.append(copy)
        gathers.append(copies)

    for copy in own[:6]:
        copy.wait()
    for slot in range(4):
        for a in range(VARS):
            blocks[slot, a, :, cells, :] = packed[slot, a].astype(jnp.float32)
    row = lax.broadcasted_iota(jnp.int32, (1, ROWS, LANES), 1)
    partner[...] = jnp.where(row[0] < CX, partner[...], 0)

    def halo_copies(turn):
        east = pltpu.make_async_remote_copy(
            src_ref=east_out.at[turn],
            dst_ref=east_in.at[turn],
            send_sem=halo_send.at[turn, 0],
            recv_sem=halo_recv.at[turn, 0],
            device_id=(tm, space + 1),
            device_id_type=MESH,
        )
        west = pltpu.make_async_remote_copy(
            src_ref=west_out.at[turn],
            dst_ref=west_in.at[turn],
            send_sem=halo_send.at[turn, 1],
            recv_sem=halo_recv.at[turn, 1],
            device_id=(tm, space - 1),
            device_id_type=MESH,
        )
        return east, west

    def send_halo(turn, field):
        view = flat(field)
        for block, cell, out in ((EAST, CX - 1, east_out), (WEST, 0, west_out)):
            edge = [view[pl.ds(a * ROWS + cell, INST, stride=VARS * ROWS), :] for a in range(VARS)]
            for i in range(VARS):
                total = blocks[block, 0, i, pl.ds(cell, 1), :] * edge[0]
                for a in range(1, VARS):
                    total = total + blocks[block, a, i, pl.ds(cell, 1), :] * edge[a]
                out[turn, i] = total
        east, west = halo_copies(turn)

        @pl.when(has_next)
        def _():
            east.start()

        @pl.when(has_previous)
        def _():
            west.start()

    def take_halo(turn):
        east, west = halo_copies(turn)
        view = flat(offdiag)

        @pl.when(has_previous)
        def _():
            east.wait_recv()
            for i in range(VARS):
                at = pl.ds(i * ROWS, INST, stride=VARS * ROWS)
                view[at, :] = view[at, :] + east_in[turn, i]

        @pl.when(has_next)
        def _():
            west.wait_recv()
            for i in range(VARS):
                at = pl.ds(i * ROWS + CX - 1, INST, stride=VARS * ROWS)
                view[at, :] = view[at, :] + west_in[turn, i]

    def couple(field):
        @pl.loop(0, INST // BLOCK)
        def _(n):
            at = pl.ds(n * BLOCK, BLOCK)
            state = [field[at, a] for a in range(VARS)]
            where_from = jnp.broadcast_to(partner[...][None], (BLOCK, ROWS, LANES))
            for i in range(VARS):
                terms = []
                for block in (EAST, WEST, PAIR):
                    total = blocks[block, 0, i][None] * state[0]
                    for a in range(1, VARS):
                        total = total + blocks[block, a, i][None] * state[a]
                    terms.append(total)
                east = jnp.where(row == 0, 0.0, pltpu.roll(terms[0], 1, 1))
                west = jnp.where(row == CX - 1, 0.0, pltpu.roll(terms[1], ROWS - 1, 1))
                pair = jnp.take_along_axis(terms[2], where_from, axis=1, mode="promise_in_bounds")
                offdiag[at, i] = east + west + pair

        weights = time_weights()

        @pl.loop(0, VARS)
        def _(i):
            offdiag[:, i] = offdiag[:, i] + scale[...][None] * cyclic(weights, field[:, i])

    def solve(n, to):
        at = pl.ds(n * BLOCK, BLOCK)
        rest = [source[at, a] - offdiag[at, a] for a in range(VARS)]
        for i in range(VARS):
            total = blocks[INV, 0, i][None] * rest[0]
            for a in range(1, VARS):
                total = total + blocks[INV, a, i][None] * rest[a]
            to[at, i] = total

    own[6].wait()
    for copy in gathers[0]:
        copy.wait_recv()
    send_halo(0, first)
    couple(first)
    take_halo(0)
    own[7].wait()
    for copy in gathers[1]:
        copy.wait_recv()

    @pl.loop(0, INST // BLOCK)
    def _(n):
        solve(n, second)

    send_halo(1, second)
    couple(second)
    take_halo(1)

    def back(peer):
        return pltpu.make_async_remote_copy(
            src_ref=result.at[pl.ds(peer * OWN, OWN), :, cells, :],
            dst_ref=out_hbm.at[:, :, :, columns(tm)],
            send_sem=back_send.at[peer],
            recv_sem=back_recv.at[tm],
            device_id=(peer, space),
            device_id_type=MESH,
        )

    own_back = pltpu.make_async_copy(
        result.at[pl.ds(tm * OWN, OWN), :, cells, :], out_hbm.at[:, :, :, columns(tm)], local_sem.at[0]
    )
    group = BLOCK // OWN

    @pl.loop(0, TM // group)
    def _(step):
        n = lax.rem(tm // group + step + 2, TM // group)
        solve(n, result)
        for k in range(group):
            peer = n * group + k

            @pl.when(peer != tm)
            def _():
                back(peer).start()

            @pl.when(peer == tm)
            def _():
                own_back.start()

    for copies in gathers:
        for copy in copies:
            copy.wait_send()
    for turn in range(2):
        east, west = halo_copies(turn)

        @pl.when(has_next)
        def _():
            east.wait_send()

        @pl.when(has_previous)
        def _():
            west.wait_send()

    own_back.wait()

    @pl.loop(0, TM)
    def _(peer):
        @pl.when(peer != tm)
        def _():
            back(peer).wait_send()
            pltpu.make_async_remote_copy(
                src_ref=result.at[pl.ds(0, OWN), :, cells, :],
                dst_ref=out_hbm.at[:, :, :, columns(peer)],
                send_sem=back_send.at[peer],
                recv_sem=back_recv.at[peer],
                device_id=(peer, space),
                device_id_type=MESH,
            ).wait_recv()


def local(
    adjoint_start, source, inv_diagonal, east_block, west_block, pair_block, time_scale, partner
):
    f32 = jnp.float32
    field = pltpu.VMEM((INST, VARS, ROWS, LANES), f32)
    halo = pltpu.VMEM((2, VARS, INST, LANES), f32)
    dma = pltpu.SemaphoreType.DMA
    return pl.pallas_call(
        kernel,
        out_shape=jax.ShapeDtypeStruct(adjoint_start.shape, f32),
        in_specs=[pl.BlockSpec(memory_space=pl.ANY)] * 8,
        out_specs=pl.BlockSpec(memory_space=pl.ANY),
        scratch_shapes=[
            field,
            field,
            field,
            field,
            field,
            pltpu.VMEM((4, VARS, VARS, CX, LANES), jnp.bfloat16),
            pltpu.VMEM((4, VARS, VARS, ROWS, LANES), f32),
            pltpu.VMEM((ROWS, LANES), f32),
            pltpu.VMEM((ROWS, LANES), jnp.int32),
            halo,
            halo,
            halo,
            halo,
            dma((8,)),
            dma((2, TM)),
            dma((2, TM)),
            dma((2, 2)),
            dma((2, 2)),
            dma((TM,)),
            dma((TM,)),
        ],
        compiler_params=pltpu.CompilerParams(
            collective_id=0, has_side_effects=True, vmem_limit_bytes=32 << 20
        ),
    )(adjoint_start, source, inv_diagonal, east_block, west_block, pair_block, time_scale, partner)


def solution(mesh):
    return jax.shard_map(
        local,
        mesh=mesh,
        in_specs=(
            P("tm", None, "space", None),
            P("tm", None, "space", None),
            P(None, None, "space", None),
            P(None, None, "space", None),
            P(None, None, "space", None),
            P(None, None, "space", None),
            P("space", None),
            P("space", None),
        ),
        out_specs=P("tm", None, "space", None),
        check_vma=False,
    )
```
